32 devices in a mesh: dp: 4 (over x, core), expert: 8 (over z, y).
Axes of the slice: x: 2, y: 2, z: 4, core: 2. Of those that a mesh axis runs over, the one named last changes fastest.
Arguments:
- tokens: bfloat16 [256, 4096], P(('dp', 'expert')), may hold values from -6 to 6
- expert_ids: int32 [256, 8], P(('dp', 'expert')), may hold values from 0 to 31, all different within a row; in each aligned block of 8 rows (0 to 7, 8 to 15, ...) at most 4 rows name the same one
- gate_weights: float32 [256, 8], P(('dp', 'expert')), may hold values from 0.1 to 1
- gate_weight: bfloat16 [4096, 14336], P('dp', 'expert'), may hold values from -0.09375 to 0.09375
- up_weight: bfloat16 [4096, 14336], P('dp', 'expert'), may hold values from -0.09375 to 0.09375
- down_weight: bfloat16 [14336, 4096], P('expert', 'dp'), may hold values from -0.125 to 0.125
- expert_gain: float32 [4, 14336], P('dp', 'expert'), may hold values from 0.5 to 2
Outputs:
- mixed: bfloat16 [256, 4096], P(('dp', 'expert'))
The draws below stay inside these ranges and needn't reach their ends.
Inputs may be any that keep to these rules, and one draw needn't show every extreme that they name: `expert_ids`: each row names 8 different experts. Among the 8 rows of one device no expert is named more than 4 times, a bound that some block reaches.
All inputs are finite; a program needn't handle non-finite values.
Results may differ from the reference program's by a relative error of at most 0.0055.
Values may be sent and summed in bfloat16 or wider, within the bound.
A program may use at most 128 MiB of HBM per device.

```python
import math
import jax
import jax.numpy as jnp
import numpy as np
from jax import lax

D = 4096
FF = 14336
EH = 1792
TOP = 8
TOK_DEV = 8
COPIES = 4
EXPERTS = 32
CAP = 4
TOKENS = 256
N_EXPERT = 8


def block_scale(key, dims, split, least, largest):
    factor_of, own = 1.0, jax.random.fold_in(key, 6)
    for position, blocks in split:
        steps = jnp.exp(jax.random.uniform(jax.random.fold_in(own, position), (blocks,), jnp.float32, least / len(split), largest / len(split)))
        factor_of = factor_of * jnp.repeat(steps, dims[position] // blocks).reshape([-1 if axis == position else 1 for axis in range(len(dims))])
    return factor_of


def assign_block(own_key, own, number, rows, count, top, most, skew):
    sequence = jax.random.permutation(own_key, count)
    heavy_load, usual = shares(count, rows * top, most, skew, True), shares(count, rows * top, most, skew, False)
    places = jnp.arange(count)

    def named(tallies, rotation):
        used = int((tallies > 0).sum())
        fixed = max(1, used // 4)
        passed = fixed + (places - fixed + rotation * (used - fixed)) % max(1, count - fixed)
        return jnp.zeros((count,), jnp.int32).at[sequence[jnp.where(places < fixed, places, passed)]].set(jnp.asarray(tallies, jnp.int32))

    tallies = jnp.where(number % 4 == 0, named(heavy_load, number // 4), named(usual, number - number // 4 - 1))
    mixed = jax.random.permutation(jax.random.fold_in(own, 3), count)
    giver, sink = mixed[0:count // 2 * 2:2], mixed[1:count // 2 * 2:2]
    margin = jnp.minimum(tallies[giver] - 1, most - tallies[sink]) // 2
    margin = jnp.where((giver == sequence[0]) | (sink == sequence[0]) | (tallies[sink] == 0), 0, jnp.maximum(margin, 0))
    passed = jax.random.randint(jax.random.fold_in(own, 4), (count // 2,), 0, 1 << 20) % (margin + 1)
    tallies = tallies.at[giver].add(-passed).at[sink].add(passed)
    members = jnp.searchsorted(jnp.cumsum(tallies), jnp.arange(rows * top), side="right").astype(jnp.int32)
    grid = members.reshape(top, rows).T
    grid = grid[jax.random.permutation(jax.random.fold_in(own, 1), rows)]
    rotation = jax.random.randint(jax.random.fold_in(own, 2), (rows, 1), 0, top)
    return jnp.take_along_axis(grid, (jnp.arange(top)[None, :] + rotation) % top, axis=1)


def shares(count, total, most, lean, full):
    loads = [(1 << 20) // math.isqrt(rank ** lean) + 1 for rank in range(1, count + 1)]
    largest = most if full else min(most, max(-(-total // count), total * loads[0] // sum(loads)))
    least = 1 if total - largest >= count - 1 else 0
    given, rest = [largest] + [least] * (count - 1), total - largest - least * (count - 1)
    while rest > 0:
        free = [i for i in range(1, count) if given[i] < largest] or [i for i in range(1, count) if given[i] < most]
        pool, left = sum([loads[i] for i in free]), rest
        for i in free:
            extra = min(most - given[i], max(1, left * loads[i] // pool), rest)
            given[i] = given[i] + extra
            rest = rest - extra
    return np.array(given)


def noise(stream_key, shape, deviation, limit, split=(), held_as=jnp.bfloat16):
    gain = block_scale(stream_key, shape, split, -0.22, 0.18) if split else 1.0
    array = jax.random.normal(stream_key, shape, jnp.float32) * deviation * gain
    return jnp.minimum(jnp.maximum(array, -limit), limit).astype(held_as)


def setup_inputs(seed: int = 0) -> dict:
    key_list = jax.random.split(jax.random.key(seed), 8)
    tokens = noise(key_list[0], (TOKENS, D), 1.0, 6.0, ((0, 32),))
    expert_ids_keys = jax.random.split(jax.random.fold_in(key_list[1], 1), TOKENS // TOK_DEV)
    expert_ids_turns = jax.random.permutation(jax.random.fold_in(key_list[1], 3), TOKENS // TOK_DEV)
    expert_ids = jax.vmap(lambda own, number: assign_block(jax.random.fold_in(key_list[1], 2), own, number, TOK_DEV, EXPERTS, TOP, CAP, 2))(expert_ids_keys, expert_ids_turns).reshape((TOKENS, TOP))
    gate_weights = jnp.clip(jnp.exp(math.log(1.0) - 2.3025851 * jax.random.uniform(key_list[2], (TOKENS, TOP), jnp.float32) ** block_scale(key_list[2], (TOKENS, TOP), ((0, 32),), -0.2, 0.2)), 0.1, 1.0)
    gate_weight = noise(key_list[3], (D, FF), D ** -0.5, 0.09375, ((0, 4), (1, 8)))
    up_weight = noise(key_list[4], (D, FF), D ** -0.5, 0.09375, ((0, 4), (1, 8)))
    down_weight = noise(key_list[5], (FF, D), EH ** -0.5, 0.125, ((0, 8), (1, 4)))
    expert_gain = jnp.clip(jnp.exp(math.log(2.0) - 1.3862944 * jax.random.uniform(key_list[6], (COPIES, FF), jnp.float32) ** block_scale(key_list[6], (COPIES, FF), ((0, 4), (1, 8)), -0.2, 0.2)), 0.5, 2.0)
    return dict(tokens=tokens, expert_ids=expert_ids, gate_weights=gate_weights, gate_weight=gate_weight, up_weight=up_weight, down_weight=down_weight, expert_gain=expert_gain)


def reference(tokens, expert_ids, gate_weights, gate_weight, up_weight, down_weight, expert_gain):
    segments = FF // EH
    quarters = N_EXPERT // segments
    block_cols = EH // quarters
    blocks_count = TOKENS // TOK_DEV
    route_count = TOK_DEV * TOP
    block_ids = expert_ids.reshape(blocks_count, route_count)
    route_order = jnp.arange(route_count, dtype=jnp.int32)

    def block_rank(row_ids):
        earlier = (row_ids[:, None] == row_ids[None, :]) & (route_order[None, :] < route_order[:, None])
        return jnp.sum(earlier.astype(jnp.int32), axis=1)

    rank_in = jax.vmap(block_rank)(block_ids)
    owner_row = jnp.arange(blocks_count, dtype=jnp.int32)[:, None] * CAP + rank_in
    token_index = jnp.repeat(jnp.arange(TOKENS, dtype=jnp.int32), TOP).reshape(blocks_count, route_count)
    slot_token = jnp.full((EXPERTS, blocks_count * CAP), TOKENS, dtype=jnp.int32)
    slot_token = slot_token.at[block_ids, owner_row].set(token_index)
    slot_gate = jnp.zeros((EXPERTS, blocks_count * CAP), dtype=jnp.float32)
    slot_gate = slot_gate.at[block_ids, owner_row].set(gate_weights.reshape(blocks_count, route_count))
    padded = jnp.concatenate([tokens, jnp.zeros((1, D), dtype=tokens.dtype)], axis=0)

    def one_expert(running, expert):
        copy_index = (expert // segments).astype(jnp.int32)
        segment = (expert % segments).astype(jnp.int32)
        routed = padded[slot_token[expert]]
        w_gate = lax.dynamic_slice_in_dim(gate_weight, segment * EH, EH, 1)
        w_up = lax.dynamic_slice_in_dim(up_weight, segment * EH, EH, 1)
        w_down = lax.dynamic_slice_in_dim(down_weight, segment * EH, EH, 0)
        gain_row = lax.dynamic_slice(expert_gain, (copy_index, segment * EH), (1, EH))
        gate_sum = jnp.dot(routed, w_gate, preferred_element_type=jnp.float32)
        up_sum = jnp.dot(routed, w_up, preferred_element_type=jnp.float32)
        hidden = (jax.nn.silu(gate_sum) * up_sum * gain_row).astype(jnp.bfloat16)
        summed = jnp.zeros((routed.shape[0], D), dtype=jnp.float32)
        for quarter in range(quarters):
            part_out = jnp.dot(hidden[:, quarter * block_cols:(quarter + 1) * block_cols],
                               w_down[quarter * block_cols:(quarter + 1) * block_cols, :],
                               preferred_element_type=jnp.float32).astype(jnp.bfloat16)
            part_out = lax.optimization_barrier(part_out)
            summed = summed + part_out.astype(jnp.float32)
        expert_out = summed.astype(jnp.bfloat16)
        weighted = slot_gate[expert][:, None] * expert_out.astype(jnp.float32)
        running = running.at[slot_token[expert]].add(weighted)
        return running, None

    start_sum = jnp.zeros((TOKENS + 1, D), dtype=jnp.float32)
    running, _ = lax.scan(one_expert, start_sum, jnp.arange(EXPERTS, dtype=jnp.int32))
    return running[:TOKENS].astype(jnp.bfloat16)
```

```python
import functools

import jax
import jax.numpy as jnp
from jax import lax
from jax.experimental import pallas as pl
from jax.experimental.pallas import tpu as pltpu
from jax.sharding import PartitionSpec as P

FF = 14336
EH = 1792
HALVES = 2
SKEW = (0, 1, 3, 5, 6)
SIB_DTYPE = jnp.float32
MESH = pl.DeviceIdType.MESH


def kernel(cfg, tok, ids, gws, gain, gate_hbm, up_hbm, down_hbm, out,
           wg, wu, wd, tf, t1, g1, xs, coefs, pbuf, pown, sbuf, xsend, xrecv, hid, acc, ob, rb, fs, fr,
           wsem, a_s, a_r, g_s, g_r, b_s, b_r, sib_s, sib_r, x_s, x_r, h_s, h_r, hf_s, hf_r, hs_s, hs_r,
           o_s, o_r, f_s, f_r):
    N, M, T, Dc, H, J, hc, Q = cfg
    X = N // 2
    NTQ = N * T // Q
    RQ = M * NTQ
    R = RQ // N
    NQ = N // Q
    SG = M // N
    copies = N
    segs = FF // EH
    d = lax.axis_index("dp")
    s = lax.axis_index("expert")
    xx = d // 2
    cc = d % 2
    sib = xx * 2 + (1 - cc)
    seg = s // (M // segs)

    loads = []
    for j in range(J):
        cols = pl.ds(j * hc, hc)
        loads.append((
            pltpu.make_async_copy(gate_hbm.at[:, cols], wg.at[j], wsem.at[j, 0]),
            pltpu.make_async_copy(up_hbm.at[:, cols], wu.at[j], wsem.at[j, 1]),
            pltpu.make_async_copy(down_hbm.at[cols, :], wd.at[j], wsem.at[j, 2]),
        ))
    for trio in loads:
        trio[0].start()
        trio[1].start()
    for trio in loads:
        trio[2].start()

    barrier = pltpu.get_barrier_semaphore()
    for k in range(1, N):
        pl.semaphore_signal(barrier, inc=1, device_id=((d + k) % N, s), device_id_type=MESH)
    for k in range(1, M):
        pl.semaphore_signal(barrier, inc=1, device_id=(d, (s + k) % M), device_id_type=MESH)

    lane = lax.broadcasted_iota(jnp.int32, (T, 128), 1)
    ids_v = ids[...]
    gw_v = gws[...]
    route = jnp.zeros((T, 128), jnp.float32)
    for k in range(ids_v.shape[1]):
        route = route + jnp.where(lane == ids_v[:, k:k + 1], gw_v[:, k:k + 1], 0.0)
    for p in range(N):
        tf[p, :, 0:Dc] = tok[:, p * Dc:(p + 1) * Dc].astype(jnp.float32)
        tf[p, :, Dc:Dc + 128] = route

    pl.semaphore_wait(barrier, N - 1 + M - 1)

    first = []
    for k in range(1, N):
        p = (d + k) % N
        c1 = pltpu.make_async_remote_copy(tf.at[p], t1.at[d], a_s.at[k - 1], a_r.at[k - 1],
                                          device_id=(p, s), device_id_type=MESH)
        c1.start()
        first.append(c1)
    second = []
    for k in range(1, N):
        p = (d + k) % N
        c2 = pltpu.make_async_remote_copy(gain, g1.at[d], g_s.at[k - 1], g_r.at[k - 1],
                                          device_id=(p, s), device_id_type=MESH)
        c2.start()
        second.append(c2)
    t1[d] = tf[d]
    g1[d] = gain[...]
    for c1 in first:
        c1.wait()

    bsend = []
    for q in range(Q):
        for r in range(NQ):
            pass
        v = t1[q * NQ:(q + 1) * NQ].reshape(NTQ, Dc + 128)
        w = v[:, Dc:]
        hi = w.astype(jnp.bfloat16)
        lo = (w - hi.astype(jnp.float32)).astype(jnp.bfloat16)
        xs[q, s, :, 0:Dc] = v[:, 0:Dc].astype(jnp.bfloat16)
        xs[q, s, :, Dc:Dc + 128] = hi
        xs[q, s, :, Dc + 128:] = lo
        for k in range(1, M):
            c = pltpu.make_async_remote_copy(xs.at[q, s], xs.at[q, s], b_s.at[q, k - 1], b_r.at[q, k - 1],
                                             device_id=(d, (s + k) % M), device_id_type=MESH)
            c.start()
            bsend.append(c)
    for c2 in second:
        c2.wait()

    sends = []

    def start_half(q):
        for k in range(M - 1):
            bsend[q * (M - 1) + k].wait_recv()
        w = xs[q, pl.ds(d * SG, SG), :, Dc:].reshape(R, 256)
        w = w[:, :128].astype(jnp.float32) + w[:, 128:].astype(jnp.float32)
        ln = lax.broadcasted_iota(jnp.int32, (R, 128), 1)
        for c in range(copies):
            one = jnp.sum(jnp.where(ln == c * segs + seg, w, 0.0), axis=1, keepdims=True)
            coefs[q, c] = jnp.broadcast_to(one, (R, 128))
        acc[q] = jnp.zeros((RQ, Dc), jnp.float32)

    def stage_a(q, j):
        u = q * J + j
        if j == 0:
            start_half(q)
        if q == 0:
            loads[j][0].wait()
            loads[j][1].wait()
        lhs = xs[q, :, :, 0:Dc].reshape(RQ, Dc)
        for i, mat in enumerate((wg, wu)):
            res = jnp.dot(lhs, mat[j], preferred_element_type=jnp.float32)
            res = res.reshape(X, 2, R, hc)
            for c in range(2):
                pown[u, c, :, i] = res[:, c]
        if SIB_DTYPE == jnp.float32:
            src = pown.at[u, 1 - cc]
        else:
            pbuf[u] = pown[u, 1 - cc].astype(SIB_DTYPE)
            src = pbuf.at[u]
        c = pltpu.make_async_remote_copy(src, sbuf.at[u], sib_s.at[u], sib_r.at[u],
                                         device_id=(sib, s), device_id_type=MESH)
        c.start()
        sends.append(c)
        return c

    def stage_b(u, sibc):
        sibc.wait_recv()
        cs = []
        for k in range(1, X):
            x2 = (xx + k) % X
            xsend[u, k - 1] = (pown[u, cc, x2] + sbuf[u, x2].astype(jnp.float32)).astype(jnp.bfloat16)
            c = pltpu.make_async_remote_copy(xsend.at[u, k - 1], xrecv.at[u, k - 1], x_s.at[u, k - 1],
                                             x_r.at[u, k - 1], device_id=(x2 * 2 + cc, s), device_id_type=MESH)
            c.start()
            cs.append(c)
            sends.append(c)
        return cs

    def stage_c(q, j, xcs):
        u = q * J + j
        tot = pown[u, cc, xx] + sbuf[u, xx].astype(jnp.float32)
        for k in range(1, X):
            xcs[k - 1].wait_recv()
            tot = tot + xrecv[u, k - 1].astype(jnp.float32)
        g = tot[0]
        up = tot[1]
        cf = jnp.zeros((R, hc), jnp.float32)
        for c in range(copies):
            cf = cf + coefs[q, c][:, 0:1] * g1[c, :, j * hc:(j + 1) * hc]
        hid[u, d] = ((g / (1.0 + jnp.exp(-g))) * up * cf).astype(jnp.bfloat16)
        cs = []
        for k in range(1, X):
            x2 = (xx + k) % X
            c = pltpu.make_async_remote_copy(hid.at[u, d], hid.at[u, d], h_s.at[u, k - 1], h_r.at[u, k - 1],
                                             device_id=(x2 * 2 + cc, s), device_id_type=MESH)
            c.start()
            cs.append(c)
            sends.append(c)
        c = pltpu.make_async_remote_copy(hid.at[u, d], hid.at[u, d], hs_s.at[u], hs_r.at[u],
                                         device_id=(sib, s), device_id_type=MESH)
        c.start()
        sends.append(c)
        return cs, c

    def stage_d(u, hcs):
        fw = []
        for k in range(1, X):
            x2 = (xx + X - k) % X
            hcs[k - 1].wait_recv()
            slot = hid.at[u, x2 * 2 + cc]
            c = pltpu.make_async_remote_copy(slot, slot, hf_s.at[u, k - 1], hf_r.at[u, k - 1],
                                             device_id=(sib, s), device_id_type=MESH)
            c.start()
            fw.append(c)
            sends.append(c)
        return fw

    def stage_e(q, j, own, fw):
        u = q * J + j
        own.wait_recv()
        for c in fw:
            c.wait_recv()
        if q == 0:
            loads[j][2].wait()
        h = hid[u].reshape(RQ, hc)
        acc[q] += jnp.dot(h, wd[j], preferred_element_type=jnp.float32)

    def stage_f(q):
        ob[q] = acc[q].reshape(M, NTQ, Dc).astype(jnp.bfloat16)
        cs = []
        for k in range(1, M):
            p = (s + k) % M
            c = pltpu.make_async_remote_copy(ob.at[q, p], rb.at[q, k - 1], o_s.at[q, k - 1], o_r.at[q, k - 1],
                                             device_id=(d, p), device_id_type=MESH)
            c.start()
            cs.append(c)
            sends.append(c)
        return cs

    def final_copy(p):
        return pltpu.make_async_remote_copy(fs.at[p], fr.at[d], f_s.at[p], f_r.at[d],
                                            device_id=(p, s), device_id_type=MESH)

    def stage_g(q, cs):
        tot = acc[q, pl.ds(pl.multiple_of(s * NTQ, NTQ), NTQ), :]
        for k in range(M - 1):
            cs[k].wait_recv()
            tot = tot + rb[q, k].astype(jnp.float32)
        tot = tot.reshape(NQ, T, Dc)
        for r in range(NQ):
            p = q * NQ + r
            fs[p] = tot[r]

            @pl.when(p != d)
            def _():
                final_copy(p).start()

    units = [(q, j) for q in range(Q) for j in range(J)]
    U = len(units)
    ra, rbx, rc, rd = {}, {}, {}, {}
    pending = []
    for t in range(U + SKEW[4]):
        u = t - SKEW[0]
        if 0 <= u < U:
            ra[u] = stage_a(*units[u])
        u = t - SKEW[1]
        if 0 <= u < U:
            rbx[u] = stage_b(u, ra[u])
        u = t - SKEW[2]
        if 0 <= u < U:
            rc[u] = stage_c(*units[u], rbx[u])
        u = t - SKEW[3]
        if 0 <= u < U:
            rd[u] = stage_d(u, rc[u][0])
        u = t - SKEW[4]
        if 0 <= u < U:
            q, j = units[u]
            stage_e(q, j, rc[u][1], rd[u])
            if j == J - 1:
                pending.append((q, stage_f(q)))
                if q == Q - 1:
                    for item in pending:
                        stage_g(*item)

    fr[d] = fs[d]
    for p in range(N):
        @pl.when(p != d)
        def _(p=p):
            pltpu.make_async_remote_copy(fs.at[p], fr.at[p], f_s.at[p], f_r.at[p],
                                         device_id=(p, s), device_id_type=MESH).wait()
    for p in range(N):
        out[:, p * Dc:(p + 1) * Dc] = fr[p].astype(jnp.bfloat16)
    for c in bsend:
        c.wait_send()
    for c in sends:
        c.wait_send()


def body(N, M, tokens, expert_ids, gate_weights, gate_weight, up_weight, down_weight, expert_gain):
    T, D = tokens.shape
    Dc, H = gate_weight.shape
    J = 7 if H % (7 * 256) == 0 else 1
    Q = HALVES
    hc = H // J
    X = N // 2
    U = Q * J
    NTQ = N * T // Q
    RQ = M * NTQ
    R = RQ // N
    bf, f32 = jnp.bfloat16, jnp.float32
    VM = pltpu.VMEM
    DMA = pltpu.SemaphoreType.DMA
    cfg = (N, M, T, Dc, H, J, hc, Q)
    vspec = pl.BlockSpec(memory_space=pltpu.VMEM)
    aspec = pl.BlockSpec(memory_space=pl.ANY)
    pb = (U, X, 2, R, hc) if SIB_DTYPE != f32 else (8, 128)
    return pl.pallas_call(
        functools.partial(kernel, cfg),
        out_shape=jax.ShapeDtypeStruct((T, D), bf),
        in_specs=[vspec, vspec, vspec, vspec, aspec, aspec, aspec],
        out_specs=vspec,
        scratch_shapes=[
            VM((J, Dc, hc), bf), VM((J, Dc, hc), bf), VM((J, hc, Dc), bf),
            VM((N, T, Dc + 128), f32), VM((N, T, Dc + 128), f32), VM((N, 1, H), f32),
            VM((Q, M, NTQ, Dc + 256), bf), VM((Q, N, R, 128), f32),
            VM(pb, SIB_DTYPE), VM((U, 2, X, 2, R, hc), f32), VM((U, X, 2, R, hc), SIB_DTYPE),
            VM((U, X - 1, 2, R, hc), bf), VM((U, X - 1, 2, R, hc), bf),
            VM((U, N, R, hc), bf), VM((Q, RQ, Dc), f32),
            VM((Q, M, NTQ, Dc), bf), VM((Q, M - 1, NTQ, Dc), bf),
            VM((N, T, Dc), f32), VM((N, T, Dc), f32),
            DMA((J, 3)),
            DMA((N - 1,)), DMA((N - 1,)), DMA((N - 1,)), DMA((N - 1,)),
            DMA((Q, M - 1)), DMA((Q, M - 1)),
            DMA((U,)), DMA((U,)), DMA((U, X - 1)), DMA((U, X - 1)),
            DMA((U, X - 1)), DMA((U, X - 1)), DMA((U, X - 1)), DMA((U, X - 1)), DMA((U,)), DMA((U,)),
            DMA((Q, M - 1)), DMA((Q, M - 1)), DMA((N,)), DMA((N,)),
        ],
        compiler_params=pltpu.CompilerParams(
            collective_id=0, has_side_effects=True, vmem_limit_bytes=56 * 1024 * 1024),
    )(tokens, expert_ids, gate_weights, expert_gain, gate_weight, up_weight, down_weight)


def solution(mesh):
    in_specs = (
        P(("dp", "expert"), None),
        P(("dp", "expert"), None),
        P(("dp", "expert"), None),
        P("dp", "expert"),
        P("dp", "expert"),
        P("expert", "dp"),
        P("dp", "expert"),
    )
    out_specs = P(("dp", "expert"), None)
    fn = functools.partial(body, mesh.shape["dp"], mesh.shape["expert"])
    return jax.shard_map(fn, mesh=mesh, in_specs=in_specs, out_specs=out_specs, check_vma=False)
```

```python
import functools

import jax
import jax.numpy as jnp
from jax import lax
from jax.experimental import pallas as pl
from jax.experimental.pallas import tpu as pltpu
from jax.sharding import PartitionSpec as P

FF = 14336
EH = 1792
HALVES = 2
SKEW = (0, 1, 4, 7, 8)
SIB_DTYPE = jnp.float32
MESH = pl.DeviceIdType.MESH


def kernel(cfg, tok, ids, gws, gain, gate_hbm, up_hbm, down_hbm, out,
           wg, wu, wd, tf, t1, g1, xs, coefs, pbuf, pown, sbuf, xsend, xrecv, hid, acc, ob, rb, fs, fr,
           wsem, a_s, a_r, g_s, g_r, b_s, b_r, bi_s, bi_r, sib_s, sib_r, x_s, x_r, h_s, h_r, hf_s, hf_r, hs_s, hs_r,
           o_s, o_r, f_s, f_r):
    N, M, T, Dc, H, J, hc, Q = cfg
    X = N // 2
    NTQ = N * T // Q
    RQ = M * NTQ
    R = RQ // N
    NQ = N // Q
    SG = M // N
    copies = N
    segs = FF // EH
    d = lax.axis_index("dp")
    s = lax.axis_index("expert")
    xx = d // 2
    cc = d % 2
    sib = xx * 2 + (1 - cc)
    seg = s // (M // segs)

    loads = []
    for j in range(J):
        cols = pl.ds(j * hc, hc)
        loads.append((
            pltpu.make_async_copy(gate_hbm.at[:, cols], wg.at[j], wsem.at[j, 0]),
            pltpu.make_async_copy(up_hbm.at[:, cols], wu.at[j], wsem.at[j, 1]),
            pltpu.make_async_copy(down_hbm.at[cols, :], wd.at[j], wsem.at[j, 2]),
        ))
    for trio in loads:
        trio[0].start()
        trio[1].start()
    for trio in loads:
        trio[2].start()

    barrier = pltpu.get_barrier_semaphore()
    for k in range(1, N):
        pl.semaphore_signal(barrier, inc=1, device_id=((d + k) % N, s), device_id_type=MESH)
    A = 4
    B = M // A
    a, b = s // B, s % B
    for k in range(1, A):
        pl.semaphore_signal(barrier, inc=1, device_id=(d, ((a + k) % A) * B + b), device_id_type=MESH)
    for k in range(1, B):
        pl.semaphore_signal(barrier, inc=1, device_id=(d, a * B + (b + k) % B), device_id_type=MESH)

    lane = lax.broadcasted_iota(jnp.int32, (T, 128), 1)
    ids_v = ids[...]
    gw_v = gws[...]
    route = jnp.zeros((T, 128), jnp.float32)
    for k in range(ids_v.shape[1]):
        route = route + jnp.where(lane % 64 == ids_v[:, k:k + 1], gw_v[:, k:k + 1], 0.0)
    for p in range(N):
        tf[p, :, 0:Dc] = tok[:, p * Dc:(p + 1) * Dc].astype(jnp.float32)
        tf[p, :, Dc:Dc + 128] = route

    pl.semaphore_wait(barrier, N - 1 + A - 1 + B - 1)

    first = []
    for k in range(1, N):
        p = (d + k) % N
        c1 = pltpu.make_async_remote_copy(tf.at[p], t1.at[d], a_s.at[k - 1], a_r.at[k - 1],
                                          device_id=(p, s), device_id_type=MESH)
        c1.start()
        first.append(c1)
    second = []
    for k in range(1, N):
        p = (d + k) % N
        c2 = pltpu.make_async_remote_copy(gain, g1.at[d], g_s.at[k - 1], g_r.at[k - 1],
                                          device_id=(p, s), device_id_type=MESH)
        c2.start()
        second.append(c2)
    t1[d] = tf[d]
    g1[d] = gain[...]
    for c1 in first:
        c1.wait_recv()

    sends = list(first)
    outer, inner = {}, {}

    def relay(q, ka):
        slot = xs.at[q, ((a + A - ka) % A) * B + b]
        for kb in range(1, B):
            c = pltpu.make_async_remote_copy(slot, slot, bi_s.at[q, ka, kb - 1], bi_r.at[q, ka, kb - 1],
                                             device_id=(d, a * B + (b + kb) % B), device_id_type=MESH)
            c.start()
            inner[q, ka, kb] = c
            sends.append(c)

    half_lane = lax.broadcasted_iota(jnp.int32, (NTQ, 128), 1) < 64
    for q in range(Q):
        v = t1[q * NQ:(q + 1) * NQ].reshape(NTQ, Dc + 128)
        w = v[:, Dc:]
        hi = w.astype(jnp.bfloat16).astype(jnp.float32)
        xs[q, s, :, 0:Dc] = v[:, 0:Dc].astype(jnp.bfloat16)
        xs[q, s, :, Dc:] = jnp.where(half_lane, hi, w - hi).astype(jnp.bfloat16)
        for ka in range(1, A):
            c = pltpu.make_async_remote_copy(xs.at[q, s], xs.at[q, s], b_s.at[q, ka - 1], b_r.at[q, ka - 1],
                                             device_id=(d, ((a + ka) % A) * B + b), device_id_type=MESH)
            c.start()
            outer[q, ka] = c
            sends.append(c)
        relay(q, 0)
    for q in range(Q):
        for ka in range(1, A):
            outer[q, ka].wait_recv()
            relay(q, ka)

    def start_half(q):
        for ka in range(A):
            for kb in range(1, B):
                inner[q, ka, kb].wait_recv()
        w = xs[q, pl.ds(d * SG, SG), :, Dc:].reshape(R, 128).astype(jnp.float32)
        ln = lax.broadcasted_iota(jnp.int32, (R, 128), 1)
        for c in range(copies):
            one = jnp.sum(jnp.where(ln % 64 == c * segs + seg, w, 0.0), axis=1, keepdims=True)
            coefs[q, c] = jnp.broadcast_to(one, (R, 128))
        acc[q] = jnp.zeros((RQ, Dc), jnp.float32)

    def stage_a(q, j):
        u = q * J + j
        if j == 0:
            start_half(q)
        if q == 0:
            loads[j][0].wait()
            loads[j][1].wait()
        lhs = xs[q, :, :, 0:Dc].reshape(RQ, Dc)
        for i, mat in enumerate((wg, wu)):
            res = jnp.dot(lhs, mat[j], preferred_element_type=jnp.float32)
            res = res.reshape(X, 2, R, hc)
            for c in range(2):
                pown[u, c, :, i] = res[:, c]
        if SIB_DTYPE == jnp.float32:
            src = pown.at[u, 1 - cc]
        else:
            pbuf[u] = pown[u, 1 - cc].astype(SIB_DTYPE)
            src = pbuf.at[u]
        c = pltpu.make_async_remote_copy(src, sbuf.at[u], sib_s.at[u], sib_r.at[u],
                                         device_id=(sib, s), device_id_type=MESH)
        c.start()
        sends.append(c)
        return c

    def stage_b(u, sibc):
        sibc.wait_recv()
        cs = []
        for k in range(1, X):
            x2 = (xx + k) % X
            xsend[u, k - 1] = (pown[u, cc, x2] + sbuf[u, x2].astype(jnp.float32)).astype(jnp.bfloat16)
            c = pltpu.make_async_remote_copy(xsend.at[u, k - 1], xrecv.at[u, k - 1], x_s.at[u, k - 1],
                                             x_r.at[u, k - 1], device_id=(x2 * 2 + cc, s), device_id_type=MESH)
            c.start()
            cs.append(c)
            sends.append(c)
        return cs

    def stage_c(q, j, xcs):
        u = q * J + j
        if u == 0:
            for c2 in second:
                c2.wait_recv()
        tot = pown[u, cc, xx] + sbuf[u, xx].astype(jnp.float32)
        for k in range(1, X):
            xcs[k - 1].wait_recv()
            tot = tot + xrecv[u, k - 1].astype(jnp.float32)
        g = tot[0]
        up = tot[1]
        cf = jnp.zeros((R, hc), jnp.float32)
        for c in range(copies):
            cf = cf + coefs[q, c][:, 0:1] * g1[c, :, j * hc:(j + 1) * hc]
        hid[u, d] = ((g / (1.0 + jnp.exp(-g))) * up * cf).astype(jnp.bfloat16)
        cs = []
        for k in range(1, X):
            x2 = (xx + k) % X
            c = pltpu.make_async_remote_copy(hid.at[u, d], hid.at[u, d], h_s.at[u, k - 1], h_r.at[u, k - 1],
                                             device_id=(x2 * 2 + cc, s), device_id_type=MESH)
            c.start()
            cs.append(c)
            sends.append(c)
        c = pltpu.make_async_remote_copy(hid.at[u, d], hid.at[u, d], hs_s.at[u], hs_r.at[u],
                                         device_id=(sib, s), device_id_type=MESH)
        c.start()
        sends.append(c)
        return cs, c

    def stage_d(u, hcs):
        fw = []
        for k in range(1, X):
            x2 = (xx + X - k) % X
            hcs[k - 1].wait_recv()
            slot = hid.at[u, x2 * 2 + cc]
            c = pltpu.make_async_remote_copy(slot, slot, hf_s.at[u, k - 1], hf_r.at[u, k - 1],
                                             device_id=(sib, s), device_id_type=MESH)
            c.start()
            fw.append(c)
            sends.append(c)
        return fw

    def stage_e(q, j, own, fw):
        u = q * J + j
        own.wait_recv()
        for c in fw:
            c.wait_recv()
        if q == 0:
            loads[j][2].wait()
        h = hid[u].reshape(RQ, hc)
        acc[q] += jnp.dot(h, wd[j], preferred_element_type=jnp.float32)

    def stage_f(q):
        ob[q] = acc[q].reshape(M, NTQ, Dc).astype(jnp.bfloat16)
        cs = []
        for k in range(1, M):
            p = (s + k) % M
            c = pltpu.make_async_remote_copy(ob.at[q, p], rb.at[q, k - 1], o_s.at[q, k - 1], o_r.at[q, k - 1],
                                             device_id=(d, p), device_id_type=MESH)
            c.start()
            cs.append(c)
            sends.append(c)
        return cs

    def final_copy(p):
        return pltpu.make_async_remote_copy(fs.at[p], fr.at[d], f_s.at[p], f_r.at[d],
                                            device_id=(p, s), device_id_type=MESH)

    def stage_g(q, cs):
        tot = acc[q, pl.ds(pl.multiple_of(s * NTQ, NTQ), NTQ), :]
        for k in range(M - 1):
            cs[k].wait_recv()
            tot = tot + rb[q, k].astype(jnp.float32)
        tot = tot.reshape(NQ, T, Dc)
        for r in range(NQ):
            p = q * NQ + r
            fs[p] = tot[r]

            @pl.when(p != d)
            def _():
                final_copy(p).start()

    units = [(q, j) for q in range(Q) for j in range(J)]
    U = len(units)
    ra, rbx, rc, rd = {}, {}, {}, {}
    pending = []
    for t in range(U + SKEW[4]):
        u = t - SKEW[0]
        if 0 <= u < U:
            ra[u] = stage_a(*units[u])
        u = t - SKEW[1]
        if 0 <= u < U:
            rbx[u] = stage_b(u, ra[u])
        u = t - SKEW[2]
        if 0 <= u < U:
            rc[u] = stage_c(*units[u], rbx[u])
        u = t - SKEW[3]
        if 0 <= u < U:
            rd[u] = stage_d(u, rc[u][0])
        u = t - SKEW[4]
        if 0 <= u < U:
            q, j = units[u]
            stage_e(q, j, rc[u][1], rd[u])
            if j == J - 1:
                pending.append((q, stage_f(q)))
                if q == Q - 1:
                    for item in pending:
                        stage_g(*item)

    fr[d] = fs[d]
    for p in range(N):
        @pl.when(p != d)
        def _(p=p):
            pltpu.make_async_remote_copy(fs.at[p], fr.at[p], f_s.at[p], f_r.at[p],
                                         device_id=(p, s), device_id_type=MESH).wait()
    for p in range(N):
        out[:, p * Dc:(p + 1) * Dc] = fr[p].astype(jnp.bfloat16)
    for c in second:
        c.wait_send()
    for c in sends:
        c.wait_send()


def body(N, M, tokens, expert_ids, gate_weights, gate_weight, up_weight, down_weight, expert_gain):
    T, D = tokens.shape
    Dc, H = gate_weight.shape
    J = 7 if H % (7 * 256) == 0 else 1
    Q = HALVES
    hc = H // J
    X = N // 2
    U = Q * J
    NTQ = N * T // Q
    RQ = M * NTQ
    R = RQ // N
    bf, f32 = jnp.bfloat16, jnp.float32
    VM = pltpu.VMEM
    DMA = pltpu.SemaphoreType.DMA
    cfg = (N, M, T, Dc, H, J, hc, Q)
    vspec = pl.BlockSpec(memory_space=pltpu.VMEM)
    aspec = pl.BlockSpec(memory_space=pl.ANY)
    pb = (U, X, 2, R, hc) if SIB_DTYPE != f32 else (8, 128)
    return pl.pallas_call(
        functools.partial(kernel, cfg),
        out_shape=jax.ShapeDtypeStruct((T, D), bf),
        in_specs=[vspec, vspec, vspec, vspec, aspec, aspec, aspec],
        out_specs=vspec,
        scratch_shapes=[
            VM((J, Dc, hc), bf), VM((J, Dc, hc), bf), VM((J, hc, Dc), bf),
            VM((N, T, Dc + 128), f32), VM((N, T, Dc + 128), f32), VM((N, 1, H), f32),
            VM((Q, M, NTQ, Dc + 128), bf), VM((Q, N, R, 128), f32),
            VM(pb, SIB_DTYPE), VM((U, 2, X, 2, R, hc), f32), VM((U, X, 2, R, hc), SIB_DTYPE),
            VM((U, X - 1, 2, R, hc), bf), VM((U, X - 1, 2, R, hc), bf),
            VM((U, N, R, hc), bf), VM((Q, RQ, Dc), f32),
            VM((Q, M, NTQ, Dc), bf), VM((Q, M - 1, NTQ, Dc), bf),
            VM((N, T, Dc), f32), VM((N, T, Dc), f32),
            DMA((J, 3)),
            DMA((N - 1,)), DMA((N - 1,)), DMA((N - 1,)), DMA((N - 1,)),
            DMA((Q, 3)), DMA((Q, 3)), DMA((Q, 4, M // 4 - 1)), DMA((Q, 4, M // 4 - 1)),
            DMA((U,)), DMA((U,)), DMA((U, X - 1)), DMA((U, X - 1)),
            DMA((U, X - 1)), DMA((U, X - 1)), DMA((U, X - 1)), DMA((U, X - 1)), DMA((U,)), DMA((U,)),
            DMA((Q, M - 1)), DMA((Q, M - 1)), DMA((N,)), DMA((N,)),
        ],
        compiler_params=pltpu.CompilerParams(
            collective_id=0, has_side_effects=True, vmem_limit_bytes=56 * 1024 * 1024),
    )(tokens, expert_ids, gate_weights, expert_gain, gate_weight, up_weight, down_weight)


def solution(mesh):
    in_specs = (
        P(("dp", "expert"), None),
        P(("dp", "expert"), None),
        P(("dp", "expert"), None),
        P("dp", "expert"),
        P("dp", "expert"),
        P("expert", "dp"),
        P("dp", "expert"),
    )
    out_specs = P(("dp", "expert"), None)
    fn = functools.partial(body, mesh.shape["dp"], mesh.shape["expert"])
    return jax.shard_map(fn, mesh=mesh, in_specs=in_specs, out_specs=out_specs, check_vma=False)
```
